512 devices in a mesh: rep: 2 (over x_hi), ty: 16 (over z, core), tx: 16 (over x_lo, y).
Axes of the slice: x: 4 (x_hi: 2, x_lo: 2; x = x_hi * 2 + x_lo), y: 8, z: 8, core: 2. Of those that a mesh axis runs over, the one named last changes fastest.
Arguments:
- state: float32 [2, 32, 80, 2048], P('rep', 'ty', None, 'tx'), may hold values from -6 to 6
- kappa: float32 [32, 2048], P('ty', 'tx'), may hold values from 0.02 to 0.12
- tile_face: int32 [16, 16], P('ty', 'tx'), may hold values from 0 to 5
- seam_turn: int32 [16, 16, 4], P('ty', 'tx'), may hold values from 0 to 3
- face_rate: float32 [6, 80], replicated, may hold values from 0.5 to 2
- w_in: bfloat16 [80, 512], replicated, may hold values from -0.625 to 0.625
- bias_in: float32 [512], replicated, may hold values from -6 to 6
- w_out: bfloat16 [512, 80], replicated, may hold values from -0.09375 to 0.09375
- cotangent: float32 [2, 32, 80, 2048], P('rep', 'ty', None, 'tx'), may hold values from -12 to 12
Outputs:
- final_state: float32 [2, 32, 80, 2048], P('rep', 'ty', None, 'tx')
- state_grad: float32 [2, 32, 80, 2048], P('rep', 'ty', None, 'tx')
- grad_w_in: float32 [80, 512], replicated
- grad_w_out: float32 [512, 80], replicated
- grad_bias: float32 [512], replicated
The draws below stay inside these ranges and needn't reach their ends.
Inputs may be any that keep to these rules, and one draw needn't show every extreme that they name: `seam_turn`: rotation code of each tile edge, in quarter turns, as the steps define it.
All inputs are finite; a program needn't handle non-finite values.
Results may differ from the reference program's by a relative error of at most 0.0035.
Values sent between devices are 32-bit elements; how exact they have to be, the bound alone decides.
A program may use at most 64 MiB of HBM per device.

```python
import math
from functools import partial
import jax
import jax.numpy as jnp
from jax import lax

LEV = 16
H = 512
SUBSTEPS = 4
FACES = 6
CY = 2
CX = 128
C = 80
NY = 32
NX = 2048
COLUMNS = 131072
N_REP = 2
N_TY = 16
N_TX = 16


def set_ends(drawn, rng, smallest, largest):
    extent = drawn.shape
    index_at = [jax.random.randint(jax.random.fold_in(rng, axis), (), 0, extent[axis]) for axis in range(len(extent))]
    drawn = drawn.at[tuple(index_at)].set(smallest)
    longest = extent.index(max(extent))
    index_at[longest] = (index_at[longest] + 1) % extent[longest]
    return drawn.at[tuple(index_at)].set(largest)


def level_of(rng, dims, split, least, high):
    level = 1.0
    for axis_at, blocks in split:
        steps = jax.random.uniform(jax.random.fold_in(jax.random.fold_in(rng, 6), axis_at), (blocks,), jnp.float32, least / len(split), high / len(split))
        level = level * jnp.repeat(jnp.exp(steps), dims[axis_at] // blocks).reshape((-1,) + (1,) * (len(dims) - 1 - axis_at))
    return level


def noise(stream_key, shape, scale, bound, split=(), dtype=jnp.bfloat16):
    result = jax.random.normal(stream_key, shape, jnp.float32) * scale
    if len(split) > 0:
        result = level_of(stream_key, shape, split, -0.22, 0.18) * result
    return jnp.clip(result, min=-bound, max=bound).astype(dtype)


def setup_inputs(seed: int = 0) -> dict:
    splits = jax.random.split(jax.random.key(seed), 10)
    state = noise(splits[0], (N_REP, NY, C, NX), 1.0, 6.0, ((0, 2), (1, 16), (3, 16)), jnp.float32)
    kappa = jnp.clip(jnp.exp(math.log(0.12) - 1.7917595 * jax.random.uniform(splits[1], (NY, NX), jnp.float32) ** level_of(splits[1], (NY, NX), ((0, 16), (1, 16)), -0.2, 0.2)), 0.02, 0.12)
    tile_face = set_ends(jax.random.randint(splits[2], (N_TY, N_TX), 0, FACES), jax.random.fold_in(splits[2], 1), 0, FACES - 1).astype(jnp.int32)
    seam_turn = set_ends(jax.random.randint(splits[3], (N_TY, N_TX, 4), 0, 4), jax.random.fold_in(splits[3], 1), 0, 3).astype(jnp.int32)
    face_rate = jnp.clip(jnp.exp(jax.random.uniform(splits[4], (FACES, C), jnp.float32, math.log(0.5), math.log(2.0))), 0.5, 2.0)
    w_in = noise(splits[5], (C, H), C ** -0.5, 0.625)
    bias_in = noise(splits[6], (H,), 1.0, 6.0, (), jnp.float32)
    w_out = noise(splits[7], (H, C), (8 * H) ** -0.5, 0.09375)
    cotangent = noise(splits[8], (N_REP, NY, C, NX), 2.0, 12.0, ((0, 2), (1, 16), (3, 16)), jnp.float32)
    return {"state": state, "kappa": kappa, "tile_face": tile_face, "seam_turn": seam_turn, "face_rate": face_rate, "w_in": w_in, "bias_in": bias_in, "w_out": w_out, "cotangent": cotangent}


def turn_strip(edge_strip, turn_code, inverse):
    reverse = (turn_code == 1) | (turn_code == 2)
    edge_strip = jnp.where(reverse, jnp.flip(edge_strip, -1), edge_strip)
    cosine = (turn_code == 0).astype(jnp.float32) - (turn_code == 2).astype(jnp.float32)
    sine_part = (turn_code == 1).astype(jnp.float32) - (turn_code == 3).astype(jnp.float32)
    if inverse:
        sine_part = -sine_part
    zonal_wind = edge_strip[..., :LEV, :]
    meridional = edge_strip[..., LEV:2 * LEV, :]
    others = edge_strip[..., 2 * LEV:, :]
    return jnp.concatenate([cosine * zonal_wind - sine_part * meridional, sine_part * zonal_wind + cosine * meridional, others], axis=-2)

def stencil_sum(field, northern, southern, western, eastern):
    from_above = jnp.concatenate([northern[..., None, :, :], field[..., :-1, :, :]], axis=-3)
    from_below = jnp.concatenate([field[..., 1:, :, :], southern[..., None, :, :]], axis=-3)
    from_left = jnp.concatenate([jnp.swapaxes(western, -1, -2)[..., None], field[..., :-1]], axis=-1)
    from_right = jnp.concatenate([field[..., 1:], jnp.swapaxes(eastern, -1, -2)[..., None]], axis=-1)
    return from_above + from_below + from_left + from_right - 4.0 * field

def edge_code(turns, number):
    return turns[:, :, number][None, :, :, None, None]

def laplace(blocks, turns):
    northern = turn_strip(jnp.roll(blocks[..., -1, :, :], 1, axis=1), edge_code(turns, 0), False)
    southern = turn_strip(jnp.roll(blocks[..., 0, :, :], -1, axis=1), edge_code(turns, 1), False)
    western = turn_strip(jnp.swapaxes(jnp.roll(blocks[..., -1], 1, axis=2), -1, -2), edge_code(turns, 2), False)
    eastern = turn_strip(jnp.swapaxes(jnp.roll(blocks[..., 0], -1, axis=2), -1, -2), edge_code(turns, 3), False)
    return stencil_sum(blocks, northern, southern, western, eastern)

def to_blocks(field):
    replicas = field.shape[0]
    return field.reshape(replicas, N_TY, CY, C, N_TX, CX).transpose(0, 1, 4, 2, 3, 5)

def from_blocks(blocks):
    replicas = blocks.shape[0]
    return blocks.transpose(0, 1, 3, 4, 2, 5).reshape(replicas, N_TY * CY, C, N_TX * CX)

def mix(form, left, right):
    return jnp.einsum(form, left.astype(jnp.float32), right.astype(jnp.float32), precision=lax.Precision.HIGHEST)

def column_forward(inputs, w_in, bias_in, w_out):
    hidden_z = mix('ch,ycx->yhx', w_in, inputs) + bias_in[None, :, None]
    hidden = (hidden_z * jax.nn.sigmoid(hidden_z)).astype(jnp.bfloat16)
    return mix('hc,yhx->ycx', w_out, hidden)

def column_backward(totals, pair, w_in, bias_in, w_out):
    inputs, grad_cols = pair
    hidden_z = mix('ch,ycx->yhx', w_in, inputs) + bias_in[None, :, None]
    squashed = jax.nn.sigmoid(hidden_z)
    hidden = (hidden_z * squashed).astype(jnp.bfloat16)
    cot_b = grad_cols.astype(jnp.bfloat16)
    gate_grad = mix('hc,ycx->yhx', w_out, cot_b) * squashed * (1.0 + hidden_z * (1.0 - squashed))
    gate_b = gate_grad.astype(jnp.bfloat16)
    dw_in = mix('ycx,yhx->ch', inputs, gate_b)
    dw_out = mix('yhx,ycx->hc', hidden, cot_b)
    dbias = lax.optimization_barrier(jnp.sum(gate_grad, axis=(0, 2)))
    back = mix('ch,yhx->ycx', w_in, gate_b)
    return ((totals[0] + dw_in, totals[1] + dw_out, totals[2] + dbias), back)

def reference(state, kappa, tile_face, seam_turn, face_rate, w_in, bias_in, w_out, cotangent):
    rate = face_rate[tile_face]
    kappa_blocks = kappa.reshape(N_TY, CY, N_TX, CX).transpose(0, 2, 1, 3)
    coef = kappa_blocks[None, :, :, :, None, :] * rate[None, :, :, None, :, None]
    tiles_all = N_REP * N_TY * N_TX
    forward_fn = partial(column_forward, w_in=w_in, bias_in=bias_in, w_out=w_out)
    backward_fn = partial(column_backward, w_in=w_in, bias_in=bias_in, w_out=w_out)
    field = to_blocks(state)
    saved = []
    for substep in range(SUBSTEPS):
        pre = field + coef * laplace(field, seam_turn)
        inputs = pre.astype(jnp.bfloat16)
        added = lax.map(forward_fn, inputs.reshape(tiles_all, CY, C, CX))
        field = pre + added.reshape(pre.shape)
        saved.append(inputs)
    final_state = from_blocks(field)
    grad = to_blocks(cotangent)
    totals = (jnp.zeros((C, H), jnp.float32), jnp.zeros((H, C), jnp.float32), jnp.zeros((H,), jnp.float32))
    for substep in reversed(range(SUBSTEPS)):
        pair = (saved[substep].reshape(tiles_all, CY, C, CX), grad.reshape(tiles_all, CY, C, CX))
        totals, back = lax.scan(backward_fn, totals, pair)
        pre_grad = grad + back.reshape(grad.shape)
        spread = jax.vjp(partial(laplace, turns=seam_turn), pre_grad)[1](coef * pre_grad)[0]
        grad = pre_grad + spread
    factor = 1.0 / math.sqrt(COLUMNS)
    return (final_state, from_blocks(grad), totals[0] * factor, totals[1] * factor, totals[2] * factor)
```

```python
import functools
import math

import jax
import jax.numpy as jnp
from jax import lax
from jax.experimental import pallas as pl
from jax.experimental.pallas import tpu as pltpu
from jax.sharding import PartitionSpec as P

LEV = 16
SUBSTEPS = 4
C = 80
X = 128
HID = 512
KA = 96
RED = 96
PIECE = 16
OWNERS = RED // PIECE
MESH = pl.DeviceIdType.MESH
F32 = jnp.float32
BF16 = jnp.bfloat16


def places():
    r, t, c = lax.axis_index("rep"), lax.axis_index("ty"), lax.axis_index("tx")
    return r, t, c, t % 2, 2 * r + c // 8, c % 8, t // 2


def at_core():
    r, t, c, core, x, y, z = places()
    return (r, t + 1 - 2 * core, c)


def at_x(j):
    r, t, c, core, x, y, z = places()
    xx = (x + j) % 4
    return (xx // 2, t, (xx % 2) * 8 + y)


def at_y(j):
    r, t, c, core, x, y, z = places()
    return (r, t, (c // 8) * 8 + (y + j) % 8)


def at_z(j):
    r, t, c, core, x, y, z = places()
    return (r, ((z + j) % 8) * 2 + core, c)


def beside():
    r, t, c = places()[:3]
    return (
        (r, (t + 15) % 16, c),
        (r, (t + 1) % 16, c),
        (r, t, (c + 15) % 16),
        (r, t, (c + 1) % 16),
    )


def corners():
    r, t, c = places()[:3]
    return [(r, (t + dt) % 16, (c + dc) % 16) for dt in (15, 1) for dc in (15, 1)]


def remote(src, dst, send, recv, device):
    return pltpu.make_async_remote_copy(
        src_ref=src, dst_ref=dst, send_sem=send, recv_sem=recv, device_id=device, device_id_type=MESH
    )


def lanes(shape=(8, X)):
    return lax.broadcasted_iota(jnp.int32, shape, 1)


def flip_lanes(block):
    index = X - 1 - lanes(block.shape)
    return jnp.take_along_axis(block, index, axis=1, mode="promise_in_bounds")


def code_parts(seams, k):
    code = jnp.broadcast_to(seams[:, k : k + 1], (8, X))
    one = (code > 0.5) & (code < 1.5)
    two = (code > 1.5) & (code < 2.5)
    rev = jnp.where(one | two, 1.0, 0.0)
    cos = jnp.where(code < 0.5, 1.0, 0.0) - jnp.where(two, 1.0, 0.0)
    sin = jnp.where(one, 1.0, 0.0) - jnp.where(code > 2.5, 1.0, 0.0)
    return rev, cos, sin


def turn_row(row, parts, inverse):
    rev, cos, sin = parts
    if inverse:
        sin = -sin
    mask = rev > 0.5
    blocks = []
    for k in range(C // 8):
        block = row[8 * k : 8 * k + 8]
        blocks.append(jnp.where(mask, flip_lanes(block), block))
    u, v = blocks[0:2], blocks[2:4]
    new_u = [cos * a - sin * b for a, b in zip(u, v)]
    new_v = [sin * a + cos * b for a, b in zip(u, v)]
    return jnp.concatenate(new_u + new_v + blocks[4:], axis=0)


def pack(rows):
    lane = lanes()
    packed = jnp.zeros((8, X), F32)
    for y in range(2):
        for k in range(C // 8):
            place = 64 * y + 2 * k
            moved = pltpu.roll(rows[y][8 * k : 8 * k + 8], (place + 1) % X, 1)
            packed = jnp.where((lane == place) | (lane == place + 1), moved, packed)
    return packed


def swap_sides(from_west, from_east):
    odd = lanes() % 2 == 1
    return jnp.where(odd, pltpu.roll(from_west, 1, 1), pltpu.roll(from_east, X - 1, 1))


def turn_pack(packed, tables, inverse):
    return spin_pack(jnp.where(tables[0] > 0.5, pltpu.roll(packed, 64, 1), packed), tables, inverse)


def spin_pack(packed, tables, inverse):
    rev, cos, sin_u, sin_v = tables
    spin = sin_v * pltpu.roll(packed, 4, 1) - sin_u * pltpu.roll(packed, X - 4, 1)
    return cos * packed - spin if inverse else cos * packed + spin


def by_side(west, east):
    odd = lanes() % 2 == 1
    return [jnp.where(odd, w, e) for w, e in zip(west, east)]


def pack_tables(west, east):
    return spread_tables(*by_side(west, east))


def spread_tables(rev, cos, sin):
    lane = lanes()
    at = lane % 64
    zero = jnp.zeros((8, X), F32)
    cos = jnp.where(at < 8, cos, zero + 1.0)
    return rev, cos, jnp.where(at < 4, sin, zero), jnp.where((at >= 4) & (at < 8), sin, zero)


def seconds(rows):
    first = lanes((C, X)) == 0
    return [jnp.where(first, pltpu.roll(row, X - 1, 1), pltpu.roll(row, 1, 1)) for row in rows]


def ends_beyond(north_pack, south_pack, tables):
    lane = lanes()
    wests = jnp.where(lane >= 64, north_pack[0], south_pack[0])
    easts = jnp.where(lane >= 64, north_pack[1], south_pack[1])
    rev = tables[0] > 0.5
    at_west = jnp.where(rev, pltpu.roll(wests, 64, 1), pltpu.roll(wests, 65, 1))
    at_east = jnp.where(rev, pltpu.roll(easts, 64, 1), pltpu.roll(easts, 63, 1))
    valid = lane % 64 < 2 * (C // 8)
    picked = jnp.where(valid, jnp.where(lane % 2 == 1, at_west, at_east), 0.0)
    return spin_pack(picked, tables, False)


def ends_back(north_pack, south_pack):
    lane = lanes()
    wests = jnp.where(lane >= 64, north_pack[0], south_pack[0])
    easts = jnp.where(lane >= 64, north_pack[1], south_pack[1])
    picked = jnp.where(lane % 2 == 1, pltpu.roll(wests, 65, 1), pltpu.roll(easts, 63, 1))
    return jnp.where(lane % 64 < 2 * (C // 8), picked, 0.0)


def unfold(packed):
    return jnp.concatenate(
        [packed] + [pltpu.roll(packed, X - 2 * k, 1) for k in range(1, C // 8)], axis=0
    )


def fold(columns):
    at = lanes() % 64
    packed = jnp.where(at < 2, columns[:8], 0.0)
    for k in range(1, C // 8):
        moved = pltpu.roll(columns[8 * k : 8 * k + 8], 2 * k, 1)
        packed = jnp.where((at == 2 * k) | (at == 2 * k + 1), moved, packed)
    return packed


def edges(packed, y):
    lane = lanes()
    mask = (lane == 0) | (lane == X - 1)
    zero = jnp.zeros((8, X), F32)
    return jnp.concatenate(
        [
            jnp.where(mask, pltpu.roll(packed, (X - (64 * y + 2 * k + 1)) % X, 1), zero)
            for k in range(C // 8)
        ],
        axis=0,
    )


def inner_row(row, other):
    lane = lanes((C, X))
    left = jnp.where(lane == 0, 0.0, pltpu.roll(row, 1, 1))
    right = jnp.where(lane == X - 1, 0.0, pltpu.roll(row, X - 1, 1))
    return left + right + other - 4.0 * row


def inner(rows):
    return [inner_row(rows[0], rows[1]), inner_row(rows[1], rows[0])]


def dot(a, b, dims=((1,), (0,))):
    return lax.dot_general(a, b, (dims, ((), ())), preferred_element_type=F32)


def step_kernel(
    factor,
    *refs,
):
    operands, (final_ref, grad_ref, sums_ref), loaded, refs = refs[:9], refs[9:12], refs[12:21], refs[21:]
    face_ref, seam_ref, state_ref, cot_ref, kappa_ref, rate_ref, w_in_ref, bias_ref, w_out_t = loaded
    (
    load_sem, w_in_t, w_out_ref, coef_ref, inputs_ref, hidden_ref, slope_ref, bias_acc, acc_in, acc_out,
    row_out, col_out, row_in, col_in,
    tile_out, pair_out, tile_in, pair_in, corner_in, note_out, note_in, back_out, turned_out, turned_in, outer_slope,
    mine, half_in, x_in, tile_ref, y_in, piece_ref, z_in, all_ref, final_vmem, grad_vmem,
    row_send, row_recv, col_send, col_recv, deep_send, deep_recv, note_send, note_recv,
    core_send, core_recv, xs_send, xs_recv, ys_send, ys_recv, zs_send, zs_recv,
    yg_send, yg_recv, xg_send, xg_recv, cg_send, cg_recv, keep_sem, result_sem,
    ) = refs
    rep, ty, tx, core, x, y, z = places()
    north, south, west, east = beside()
    barrier = pltpu.get_barrier_semaphore()
    friends = [north, south, west, east] + corners() + [at_x(j) for j in range(1, 4)]
    friends += [at_y(3), at_y(5), at_z(2), at_z(6)]
    for friend in friends:
        pl.semaphore_signal(barrier, inc=1, device_id=friend, device_id_type=MESH)

    loads = [
        pltpu.make_async_copy(operand, ref, load_sem.at[n])
        for n, (operand, ref) in enumerate(zip(operands, loaded))
    ]
    for n in (2, 0, 1, 4, 5, 6, 7, 8, 3):
        loads[n].start()
    results = [
        pltpu.make_async_copy(final_vmem, final_ref.at[0], result_sem.at[0]),
        pltpu.make_async_copy(grad_vmem, grad_ref.at[0], result_sem.at[1]),
    ]
    copies = []

    def start(copy):
        copy.start()
        copies.append(copy)
        return copy

    def exchange(e, first, last):
        return [
            start(remote(col_out.at[e], col_in.at[e, 1], col_send.at[e, 0], col_recv.at[e, 1], west)),
            start(remote(col_out.at[e], col_in.at[e, 0], col_send.at[e, 1], col_recv.at[e, 0], east)),
            start(remote(first, row_in.at[e, 1], row_send.at[e, 0], row_recv.at[e, 1], north)),
            start(remote(last, row_in.at[e, 0], row_send.at[e, 1], row_recv.at[e, 0], south)),
        ]

    def arrived(flights):
        for flight in flights:
            flight.wait_recv()

    def deep_tiles(d, tiles):
        return [
            start(remote(tiles[n], tile_in.at[d, 1 - n], deep_send.at[d, n], deep_recv.at[d, 1 - n], device))
            for n, device in enumerate((north, south))
        ]

    def deep_corners(d, corner_out, corner_in):
        return [
            start(remote(corner_out, corner_in.at[3 - n], deep_send.at[d, 4 + n], deep_recv.at[d, 7 - n], device))
            for n, device in enumerate(corners())
        ]

    def deep_sides(d):
        return [
            start(remote(pair_out.at[d], pair_in.at[d, 1 - n], deep_send.at[d, 2 + n], deep_recv.at[d, 3 - n], device))
            for n, device in enumerate((west, east))
        ]

    loads[2].wait()
    field = [state_ref[0, 0], state_ref[0, 1]]
    pair_out[0, 0] = pack(field)
    pair_out[0, 1] = pack(seconds(field))
    pl.semaphore_wait(barrier, len(friends))
    flights = deep_corners(0, pair_out.at[0, 0], corner_in.at[0])
    flights += deep_tiles(0, [state_ref.at[0]] * 2) + deep_sides(0)

    for n in (0, 1, 4, 5, 6, 7, 8):
        loads[n].wait()
    seams = seam_ref[0].astype(F32)
    parts = [code_parts(seams, k) for k in range(4)]
    tables = pack_tables(parts[2], parts[3])
    rate_row = jnp.zeros((1, C), F32)
    face_here = jnp.broadcast_to(face_ref[...], (1, C))
    for face in range(rate_ref.shape[0]):
        rate_row = rate_row + jnp.where(face_here == face, 1.0, 0.0) * rate_ref[face : face + 1, :]
    rate = jnp.broadcast_to(rate_row, (X, C)).T
    coefs = [rate * kappa_ref[k : k + 1, :] for k in range(2)]
    for k in range(2):
        coef_ref[k] = coefs[k]
    note_out[0] = jnp.zeros((8, X), F32)
    note_out[0, 0:2] = kappa_ref[...]
    note_out[0, 2:3, 0:C] = rate_row
    note_out[0, 3:4, 0:4] = seams
    note_out[1] = pack(coefs)
    flights += [
        start(remote(note_out, note_in.at[n ^ 1], note_send.at[n], note_recv.at[n ^ 1], device))
        for n, device in enumerate((north, south, west, east))
    ]
    bias = bias_ref[...]
    high = bias.astype(BF16).astype(F32)
    middle = (bias - high).astype(BF16).astype(F32)
    low = bias - high - middle
    at_row = lax.broadcasted_iota(jnp.int32, (KA - C, HID), 0)
    extra = jnp.where(at_row == 0, high, jnp.where(at_row == 1, middle, jnp.where(at_row == 2, low, 0.0)))
    w_in_t[...] = jnp.concatenate([w_in_ref[...].astype(F32), extra], axis=0).T.astype(BF16)
    w_out_ref[...] = w_out_t[...].astype(F32).T.astype(BF16)
    ones = jnp.where(lax.broadcasted_iota(jnp.int32, (KA - C, 2 * X), 0) < 3, 1.0, 0.0).astype(BF16)

    def network(s, inputs, slope_at):
        width = inputs.shape[1]
        filler = jnp.concatenate([ones] * (-(-width // (2 * X))), axis=1)[:, :width]
        z_all = dot(w_in_t[...], jnp.concatenate([inputs, filler], axis=0))
        squashed = 0.5 + 0.5 * jnp.tanh(0.5 * z_all)
        silu = z_all * squashed
        hidden = silu.astype(BF16)
        if s is not None:
            inputs_ref[s] = inputs
            hidden_ref[s] = hidden
        if slope_at is not None:
            slope_at[...] = squashed + silu * (1.0 - squashed)
        return dot(w_out_t[...], hidden)

    def own_step(s, field, inside, above, below, sides):
        rims = turn_pack(sides, tables, False)
        pre = []
        for k, beyond in enumerate((above, below)):
            rim = turn_row(beyond, parts[k], False)
            pre.append(field[k] + coef_ref[k] * (inside[k] + rim + edges(rims, k)))
        added = network(s, jnp.concatenate(pre, axis=1).astype(BF16), slope_ref.at[s])
        return [pre[k] + added[:, X * k : X * k + X] for k in range(2)]

    for d in range(SUBSTEPS // 2):
        inside = inner(field)
        arrived(flights)
        if d == 0:
            codes = [[code_parts(note_in[n, 0, 3:4, 0:4], k) for k in range(4)] for n in range(4)]
            of_north, of_south, of_west, of_east = codes
            north_tables = pack_tables(of_north[2], of_north[3])
            south_tables = pack_tables(of_south[2], of_south[3])
            back_tables = pack_tables(of_west[3], of_east[2])
            upper = lanes() < 64
            end_tables = spread_tables(*[
                jnp.where(upper, a, b)
                for a, b in zip(by_side(of_west[0], of_east[0]), by_side(of_west[1], of_east[1]))
            ])
            far_coef = [
                jnp.broadcast_to(note_in[n, 0, 2:3], (X, X)).T[:C] * note_in[n, 0, 1 - n : 2 - n]
                for n in range(2)
            ]
            row_tables = spread_tables(*[jnp.where(upper, a, b) for a, b in zip(parts[0], parts[1])])
            side_coef = swap_sides(note_in[2, 1], note_in[3, 1])
        sides = swap_sides(pair_in[d, 0, 0], pair_in[d, 1, 0])
        nearer = swap_sides(pair_in[d, 0, 1], pair_in[d, 1, 1])
        up, down = tile_in[d, 0, 1], tile_in[d, 1, 0]
        up_sides = turn_pack(swap_sides(corner_in[d, 0], corner_in[d, 1]), north_tables, False)
        down_sides = turn_pack(swap_sides(corner_in[d, 2], corner_in[d, 3]), south_tables, False)
        up_pre = up + far_coef[0] * (
            inner_row(up, tile_in[d, 0, 0]) + turn_row(field[0], of_north[1], False) + edges(up_sides, 1)
        )
        down_pre = down + far_coef[1] * (
            inner_row(down, tile_in[d, 1, 1]) + turn_row(field[1], of_south[0], False) + edges(down_sides, 0)
        )
        ends = ends_beyond(
            (corner_in[d, 0], corner_in[d, 1]), (corner_in[d, 2], corner_in[d, 3]), end_tables
        )
        sides_pre = sides + side_coef * (
            nearer + turn_pack(pair_out[d, 0], back_tables, False) + pltpu.roll(sides, 64, 1) + ends - 4.0 * sides
        )
        field = own_step(2 * d, field, inside, up, down, sides)
        outer = jnp.concatenate([up_pre, down_pre, unfold(sides_pre)], axis=1).astype(BF16)
        added = network(None, outer, None if 2 * d + 2 < SUBSTEPS else outer_slope)
        up = up_pre + added[:, :X]
        down = down_pre + added[:, X : 2 * X]
        sides = sides_pre + fold(added[:, 2 * X :])
        field = own_step(2 * d + 1, field, inner(field), up, down, sides)
        if 2 * d + 2 < SUBSTEPS:
            pair_out[d + 1, 0] = pack(field)
            flights = deep_corners(d + 1, pair_out.at[d + 1, 0], corner_in.at[d + 1])
            for k in range(2):
                tile_out[k] = field[k]
            flights += deep_tiles(d + 1, [tile_out] * 2)
            pair_out[d + 1, 1] = pack(seconds(field))
            flights += deep_sides(d + 1)
        else:
            for k in range(2):
                final_vmem[k] = field[k]
            results[0].start()

    loads[3].wait()
    def network_back(cot_b, slope):
        gate = dot(w_out_ref[...], cot_b) * slope
        gate_b = gate.astype(BF16)
        return gate, gate_b, dot(w_in_ref[...], gate_b)

    def own_back(s, grad):
        cot_b = jnp.concatenate(grad, axis=1).astype(BF16)
        gate, gate_b, back = network_back(cot_b, slope_ref[s])
        return [grad[k] + back[:, X * k : X * k + X] for k in range(2)], (s, cot_b, gate, gate_b)

    def gather(known):
        s, cot_b, gate, gate_b = known
        folded = gate[:, :X] + gate[:, X:]
        dw_in = dot(inputs_ref[s], gate_b, ((1,), (1,)))
        dw_out = dot(cot_b, hidden_ref[s], ((1,), (1,)))
        if s < SUBSTEPS - 1:
            folded = folded + bias_acc[...]
            dw_in = dw_in + acc_in[...]
            dw_out = dw_out + acc_out[...]
        if s > 0:
            bias_acc[...] = folded
            acc_in[...] = dw_in
            acc_out[...] = dw_out
        return folded, dw_in, dw_out

    pre_grad, known = own_back(SUBSTEPS - 1, [cot_ref[0, 0], cot_ref[0, 1]])
    weighted = [coef_ref[k] * pre_grad[k] for k in range(2)]
    packed = pack(pre_grad)
    weighted_pack = note_out[1] * packed
    own_turned = turn_pack(weighted_pack, tables, True)
    turned_out[0] = own_turned
    turned_out[1] = spin_pack(
        jnp.where(row_tables[0] > 0.5, swap_sides(weighted_pack, weighted_pack), weighted_pack), row_tables, True
    )
    flights = deep_corners(2, turned_out, turned_in)
    back_out[0, 0], back_out[0, 1] = pre_grad[0], weighted[1]
    back_out[1, 0], back_out[1, 1] = weighted[0], pre_grad[1]
    flights += deep_tiles(2, [back_out.at[0], back_out.at[1]])
    pair_out[2, 0] = packed
    pair_out[2, 1] = pack(seconds(weighted))
    flights += deep_sides(2)
    gather(known)
    inside = inner(weighted)
    to_north, to_south = [turn_row(weighted[k], parts[k], True) for k in range(2)]
    arrived(flights)
    up, down = tile_in[2, 0, 1], tile_in[2, 1, 0]
    sides = swap_sides(pair_in[2, 0, 0], pair_in[2, 1, 0])
    nearer = swap_sides(pair_in[2, 0, 1], pair_in[2, 1, 1])
    up_w, down_w, sides_w = far_coef[0] * up, far_coef[1] * down, side_coef * sides

    def spread_back(pre_grad, inside, up_w, down_w, sides_w):
        rims = turn_pack(sides_w, back_tables, True)
        beyond = [turn_row(up_w, of_north[1], True), turn_row(down_w, of_south[0], True)]
        return [pre_grad[k] + inside[k] + beyond[k] + edges(rims, k) for k in range(2)]

    grad = spread_back(pre_grad, inside, up_w, down_w, sides_w)
    up_grad = (
        up + inner_row(up_w, tile_in[2, 0, 0]) + to_north + edges(swap_sides(turned_in[0, 0], turned_in[1, 0]), 1)
    )
    down_grad = (
        down + inner_row(down_w, tile_in[2, 1, 1]) + to_south + edges(swap_sides(turned_in[2, 0], turned_in[3, 0]), 0)
    )
    ends = ends_back((turned_in[0, 1], turned_in[1, 1]), (turned_in[2, 1], turned_in[3, 1]))
    sides_grad = sides + nearer + pltpu.roll(sides_w, 64, 1) - 4.0 * sides_w + own_turned + ends
    outer_cot = jnp.concatenate([up_grad, down_grad, unfold(sides_grad)], axis=1).astype(BF16)
    pre_grad, before = own_back(SUBSTEPS - 2, grad)
    back = network_back(outer_cot, outer_slope[...])[2]
    up_w = far_coef[0] * (up_grad + back[:, :X])
    down_w = far_coef[1] * (down_grad + back[:, X : 2 * X])
    sides_w = side_coef * (sides_grad + fold(back[:, 2 * X :]))
    grad = spread_back(pre_grad, inner([coef_ref[k] * pre_grad[k] for k in range(2)]), up_w, down_w, sides_w)

    def send_back(e, weighted):
        col_out[e] = turn_pack(pack(weighted), tables, True)
        for k in range(2):
            row_out[e, k] = turn_row(weighted[k], parts[k], True)
        return exchange(e, row_out.at[e, 0], row_out.at[e, 1])

    def come_back(e, pre_grad, inside):
        arrived(flights)
        sides = swap_sides(col_in[e, 0], col_in[e, 1])
        return [pre_grad[k] + inside[k] + row_in[e, k] + edges(sides, k) for k in range(2)]

    pre_grad, known = own_back(1, grad)
    weighted = [coef_ref[k] * pre_grad[k] for k in range(2)]
    flights = send_back(1, weighted)
    gather(before)
    gather(known)
    inside = inner(weighted)
    grad = come_back(1, pre_grad, inside)
    pre_grad, known = own_back(0, grad)
    folded, dw_in, dw_out = gather(known)

    dbias = lax.dot_general(
        jnp.ones((8, X), F32), folded, (((1,), (1,)), ((), ())),
        preferred_element_type=F32, precision=lax.Precision.HIGHEST,
    )
    blank = jnp.zeros((8, X), F32)
    for i in range(4):
        cut = slice(X * i, X * i + X)
        mine[0, i] = jnp.concatenate([dw_in[:, cut], blank, blank], axis=0)
        mine[1, i] = jnp.concatenate([dw_out[:, cut], dbias[:, cut], blank], axis=0)
    core_flights = []
    for n, j in enumerate((2, 1, 3, 0)):
        tile = (x + j) % 4
        core_flights.append(
            start(remote(mine.at[1 - core, tile], half_in.at[j], core_send.at[n], core_recv.at[n], at_core()))
        )

    weighted = [coef_ref[k] * pre_grad[k] for k in range(2)]
    flights = send_back(0, weighted)
    inside = inner(weighted)

    x_flights = []
    for n, j in enumerate((2, 1, 3, 0)):
        tile = (x + j) % 4
        core_flights[n].wait_recv()
        if j:
            half_in[j] = half_in[j] + mine[core, tile]
            x_flights.append(start(remote(half_in.at[j], x_in.at[j - 1], xs_send.at[j - 1], xs_recv.at[j - 1], at_x(j))))
        else:
            total = half_in[0] + mine[core, tile]
    for flight in x_flights:
        flight.wait_recv()
    tile_ref[...] = (total + x_in[0] + x_in[1] + x_in[2]).reshape(OWNERS, PIECE, X)

    def y_copy(j):
        return remote(tile_ref.at[(y + j) % 8], y_in.at[j - 1], ys_send.at[j - 1], ys_recv.at[j - 1], at_y(j))

    def z_copy(j):
        return remote(piece_ref, z_in.at[z], zs_send.at[j - 1], zs_recv.at[j - 1], at_z(j))

    order = (4, 3, 5, 2, 6, 1, 7)
    for j in order:
        @pl.when((y + j) % 8 < OWNERS)
        def _():
            y_copy(j).start()

    grad = come_back(0, pre_grad, inside)
    for k in range(2):
        grad_vmem[k] = grad[k]
    results[1].start()
    for copy in copies:
        copy.wait_send()
    copies.clear()

    @pl.when(y < OWNERS)
    def _():
        part = tile_ref[y]
        for j in range(1, 8):
            came = y_in.at[j - 1]
            remote(came, came, ys_send.at[j - 1], ys_recv.at[j - 1], at_y(j)).wait_recv()
            part = part + y_in[j - 1]
        piece_ref[...] = part
        z_in[z] = part
        for j in order:
            z_copy(j).start()
        for j in order:
            z_copy(j).wait_recv()
        whole = z_in[0]
        for i in range(1, 8):
            whole = whole + z_in[i]
        all_ref[x, y] = whole * factor

    def yg_copy(j):
        return remote(all_ref.at[x, y], all_ref.at[x, y], yg_send.at[j - 1], yg_recv.at[j - 1], at_y(j))

    def xg_copy(j, owner):
        piece = all_ref.at[x, owner]
        return remote(piece, piece, xg_send.at[j - 1, owner], xg_recv.at[j - 1, owner], at_x(j))

    @pl.when(y < OWNERS)
    def _():
        for j in order:
            yg_copy(j).start()

    for j in (0, 1, 7, 2, 6, 3, 5, 4):
        owner = (y - j + 8) % 8

        @pl.when(owner < OWNERS)
        def _():
            if j:
                came = all_ref.at[x, owner]
                remote(came, came, yg_send.at[j - 1], yg_recv.at[j - 1], at_y(j)).wait_recv()
            for i in (2, 1, 3):
                xg_copy(i, owner).start()

        if j == 0:
            for i in order:
                @pl.when((y + i) % 8 < OWNERS)
                def _():
                    y_copy(i).wait_send()

            @pl.when(y < OWNERS)
            def _():
                for i in order:
                    z_copy(i).wait_send()

    def hand_over(n, tile):
        pltpu.make_async_copy(all_ref.at[tile], sums_ref.at[core, tile], keep_sem.at[n]).start()
        return start(remote(all_ref.at[tile], sums_ref.at[core, tile], cg_send.at[n], cg_recv.at[n], at_core()))

    cg_flights = [hand_over(0, x)]
    for j in (1, 3, 2):
        for owner in range(OWNERS):
            xg_copy(j, owner).wait_recv()
        cg_flights.append(hand_over(j, (x - j + 4) % 4))
    for j in range(1, 4):
        for owner in range(OWNERS):
            xg_copy(j, owner).wait_send()

    @pl.when(y < OWNERS)
    def _():
        for j in order:
            yg_copy(j).wait_send()

    for result in results:
        result.wait()
    for flight in cg_flights:
        flight.wait_recv()
    for j in range(4):
        tile = (x - j + 4) % 4
        pltpu.make_async_copy(all_ref.at[tile], sums_ref.at[core, tile], keep_sem.at[j]).wait()
    for copy in copies:
        copy.wait_send()


def place_kernel(final_ref, grad_ref, sums_ref, *outs):
    outs[0][...] = final_ref[...]
    outs[1][...] = grad_ref[...]
    for i in range(4):
        cut = slice(X * i, X * i + X)
        outs[2][:, cut] = sums_ref[0, i, :C]
        outs[3][:, cut] = sums_ref[1, i, :C]
        outs[4][:, cut] = sums_ref[1, i, C : C + 1]


def shards(state, kappa, tile_face, seam_turn, face_rate, w_in, bias_in, w_out, cotangent):
    vmem = pl.BlockSpec(memory_space=pltpu.VMEM)
    hbm = pl.BlockSpec(memory_space=pltpu.HBM)
    operands = (tile_face, seam_turn, state, cotangent, kappa, face_rate, w_in, bias_in[None], w_out.T)
    steps = 2
    dma = lambda *shape: pltpu.SemaphoreType.DMA(shape)
    all_columns = lax.axis_size("rep") * lax.axis_size("ty") * lax.axis_size("tx") * 2 * X
    final, grad, sums = pl.pallas_call(
        functools.partial(step_kernel, 1.0 / math.sqrt(all_columns)),
        out_shape=(
            jax.ShapeDtypeStruct(state.shape, F32),
            jax.ShapeDtypeStruct(state.shape, F32),
            jax.ShapeDtypeStruct((2, 4, OWNERS, PIECE, X), F32),
        ),
        in_specs=[hbm] * 9,
        out_specs=(hbm, hbm, hbm),
        scratch_shapes=[
            *[pltpu.VMEM(operand.shape, operand.dtype) for operand in operands],
            dma(9),
            pltpu.VMEM((HID, KA), BF16),
            pltpu.VMEM((HID, C), BF16),
            pltpu.VMEM((2, C, X), F32),
            pltpu.VMEM((SUBSTEPS, C, 2 * X), BF16),
            pltpu.VMEM((SUBSTEPS, HID, 2 * X), BF16),
            pltpu.VMEM((SUBSTEPS, HID, 2 * X), F32),
            pltpu.VMEM((HID, X), F32),
            pltpu.VMEM((C, HID), F32),
            pltpu.VMEM((C, HID), F32),
            pltpu.VMEM((steps, 2, C, X), F32),
            pltpu.VMEM((steps, 8, X), F32),
            pltpu.VMEM((steps, 2, C, X), F32),
            pltpu.VMEM((steps, 2, 8, X), F32),
            pltpu.VMEM((2, C, X), F32),
            pltpu.VMEM((3, 2, 8, X), F32),
            pltpu.VMEM((3, 2, 2, C, X), F32),
            pltpu.VMEM((3, 2, 2, 8, X), F32),
            pltpu.VMEM((2, 4, 8, X), F32),
            pltpu.VMEM((2, 8, X), F32),
            pltpu.VMEM((4, 2, 8, X), F32),
            pltpu.VMEM((2, 2, C, X), F32),
            pltpu.VMEM((2, 8, X), F32),
            pltpu.VMEM((4, 2, 8, X), F32),
            pltpu.VMEM((HID, 3 * X), F32),
            pltpu.VMEM((2, 4, RED, X), F32),
            pltpu.VMEM((4, RED, X), F32),
            pltpu.VMEM((3, RED, X), F32),
            pltpu.VMEM((OWNERS, PIECE, X), F32),
            pltpu.VMEM((7, PIECE, X), F32),
            pltpu.VMEM((PIECE, X), F32),
            pltpu.VMEM((8, PIECE, X), F32),
            pltpu.VMEM((4, OWNERS, PIECE, X), F32),
            pltpu.VMEM((2, C, X), F32),
            pltpu.VMEM((2, C, X), F32),
            dma(steps, 2), dma(steps, 2), dma(steps, 2), dma(steps, 2), dma(3, 8), dma(3, 8), dma(4), dma(4),
            dma(4), dma(4), dma(3), dma(3), dma(7), dma(7), dma(7), dma(7),
            dma(7), dma(7), dma(3, OWNERS), dma(3, OWNERS), dma(4), dma(4), dma(4), dma(2),
        ],
        compiler_params=pltpu.CompilerParams(
            collective_id=0, has_side_effects=True, vmem_limit_bytes=62 << 20
        ),
        name="training_step",
    )(*operands)
    final, grad, total_in, total_out, total_bias = pl.pallas_call(
        place_kernel,
        out_shape=(
            jax.ShapeDtypeStruct(state.shape, F32),
            jax.ShapeDtypeStruct(state.shape, F32),
            jax.ShapeDtypeStruct((C, HID), F32),
            jax.ShapeDtypeStruct((C, HID), F32),
            jax.ShapeDtypeStruct((1, HID), F32),
        ),
        name="place_results",
    )(final, grad, sums.reshape(2, 4, RED, X))
    return final, grad, total_in, total_out.T, total_bias.reshape(HID)


def solution(mesh):
    placed = (
        P("rep", "ty", None, "tx"),
        P("ty", "tx"),
        P("ty", "tx"),
        P("ty", "tx", None),
        P(),
        P(),
        P(),
        P(),
        P("rep", "ty", None, "tx"),
    )
    return jax.shard_map(
        shards,
        mesh=mesh,
        in_specs=placed,
        out_specs=(P("rep", "ty", None, "tx"), P("rep", "ty", None, "tx"), P(), P(), P()),
        check_vma=False,
    )
```
